32 devices in a mesh: row: 4 (over y, x), col: 8 (over z, core).
Axes of the slice: x: 2, y: 2, z: 4, core: 2. Of those that a mesh axis runs over, the one named last changes fastest.
Arguments:
- ancestor: float32 [24576, 24576], P('row', 'col'), may hold values from -6 to 6
- panels: float32 [4, 8, 256, 512], P(None, 'col'), may hold values from -0.125 to 0.125
- diag_inverse: float32 [4, 512, 512], P(None, 'row'), may hold values from -6 to 6
- fill_strips: int32 [4, 8], replicated, may hold values from 0 to 95, as said below
Outputs:
- upper_strips: float32 [4, 8, 256, 512], P(None, 'col')
- diagonal_blocks: float32 [4, 512, 512], P(None, 'row')
The draws below stay inside these ranges and needn't reach their ends.
Inputs may be any that keep to these rules, and one draw needn't show every extreme that they name: `fill_strips`: each row lists 8 different strips in no particular order; of the strips s with the same s // 12 a row lists at most 2, and exactly 2 for some value; of the strips with the same s // 24 it lists at most 4, and exactly that many for some value.
All inputs are finite; a program needn't handle non-finite values.
Results may differ from the reference program's by a relative error of at most 0.0001.
Values sent between devices are 32-bit elements; how exact they have to be, the bound alone decides.
A program may use at most 192 MiB of HBM per device.

```python
import jax
import jax.numpy as jnp
from jax import lax

M = 24576
W = 512
STRIP = 256
NSUP = 4
FILL_DEV = 1
FILL = 8
STRIPS = 96
N_ROW = 4


def draw_fill_strips(key, part):
    columns = FILL // FILL_DEV
    per_col = STRIPS // columns
    per_row = columns // N_ROW
    listing = []
    for supernode in range(NSUP):
        base = jax.random.fold_in(key, 211 + supernode)
        busy = jax.random.randint(jax.random.fold_in(base, 1), (), 0, N_ROW, dtype=jnp.int32)
        ids = jnp.arange(columns, dtype=jnp.int32)
        in_busy = (ids // per_row == busy).astype(jnp.int32)
        scores = jax.random.randint(jax.random.fold_in(base, 2), (columns,), 0, 65536, dtype=jnp.int32) * columns + ids
        scores = scores * (1 - in_busy) - in_busy
        emptied = lax.top_k(scores, per_row)[1].astype(jnp.int32)
        empty_mask = jnp.sum((ids[:, None] == emptied[None, :]).astype(jnp.int32), axis=1)
        counts = 1 + in_busy - empty_mask
        picks = jax.random.randint(jax.random.fold_in(base, 3), (columns, per_col), 0, 65536, dtype=jnp.int32) * per_col + jnp.arange(per_col, dtype=jnp.int32)[None, :]
        chosen = lax.top_k(picks, 2)[1].astype(jnp.int32)
        lower = jnp.min(chosen, axis=1)
        upper = jnp.max(chosen, axis=1)
        strips = jnp.stack([ids * per_col + lower, ids * per_col + upper], axis=1).reshape(-1)
        valid = jnp.stack([counts >= 1, counts >= 2], axis=1).reshape(-1).astype(jnp.int32)
        order = jnp.argsort((1 - valid) * (2 * columns) + jnp.arange(2 * columns, dtype=jnp.int32))
        sorted_strips = strips[order[:FILL]]
        before = jnp.cumsum(counts) - counts - ids
        good = jnp.logical_and(before <= 0, before + counts >= 1).astype(jnp.int32)
        anchor = jnp.argmax(good).astype(jnp.int32)
        shuffle = jax.random.permutation(jax.random.fold_in(base, 4), FILL).astype(jnp.int32)
        where_anchor = jnp.argmax((shuffle == anchor).astype(jnp.int32)).astype(jnp.int32)
        target = (anchor + FILL // 2) % FILL
        shuffle = jnp.where(ids == target, anchor, jnp.where(ids == where_anchor, shuffle[target], shuffle))
        listing.append(sorted_strips[shuffle])
    return jnp.stack(listing).astype(jnp.int32)


def steps_of(stream_key, dims, cuts, low, largest):
    loudness = 1.0
    for dim, blocks in cuts:
        steps = jax.random.uniform(jax.random.fold_in(jax.random.fold_in(stream_key, 6), dim), (blocks,), jnp.float32, low / len(cuts), largest / len(cuts))
        loudness = loudness * jnp.repeat(jnp.exp(steps), dims[dim] // blocks).reshape((-1,) + (1,) * (len(dims) - 1 - dim))
    return loudness


def gaussian(own_key, extent, scale, bound, pieces=(), kind=jnp.bfloat16):
    entries = scale * jax.random.normal(own_key, extent, jnp.float32)
    if pieces:
        entries = entries * steps_of(own_key, extent, pieces, -0.22, 0.18)
    return jnp.clip(entries, -bound, bound).astype(kind)


def setup_inputs(seed: int = 0) -> dict:
    arg_keys = jax.random.split(jax.random.key(seed), 5)
    return {
        "ancestor": gaussian(arg_keys[0], (M, M), 1.0, 6.0, ((0, 4), (1, 8)), jnp.float32),
        "panels": gaussian(arg_keys[1], (NSUP, FILL, STRIP, W), (FILL * STRIP) ** -0.5, 0.125, ((1, 8),), jnp.float32),
        "diag_inverse": gaussian(arg_keys[2], (NSUP, W, W), 1.0, 6.0, ((1, 4),), jnp.float32),
        "fill_strips": draw_fill_strips(jax.random.fold_in(arg_keys[4], 71), 0),
    }


def reference(ancestor, panels, diag_inverse, fill_strips):
    offsets = jnp.arange(STRIP, dtype=jnp.int32)
    uppers = []
    diagonals = []
    for supernode in range(NSUP):
        row_ids = (fill_strips[supernode][:, None].astype(jnp.int32) * STRIP + offsets[None, :]).reshape(-1).astype(jnp.int32)
        selected = jnp.take(jnp.take(ancestor, row_ids, axis=0), row_ids, axis=1)
        factor = panels[supernode].reshape(FILL * STRIP, W)
        upper = -jnp.dot(selected, factor, precision=lax.Precision.HIGHEST, preferred_element_type=jnp.float32)
        diagonal = diag_inverse[supernode] - jnp.dot(factor.T, upper, precision=lax.Precision.HIGHEST, preferred_element_type=jnp.float32)
        uppers.append(upper.reshape(FILL, STRIP, W))
        diagonals.append(diagonal)
    return jnp.stack(uppers), jnp.stack(diagonals)
```

```python
import functools

import jax
import jax.numpy as jnp
from jax import lax
from jax.experimental import pallas as pl
from jax.experimental.pallas import tpu as pltpu
from jax.sharding import PartitionSpec as P

MESH = pl.DeviceIdType.MESH


def split(x):
    high = x.astype(jnp.bfloat16)
    return high, (x - high.astype(jnp.float32)).astype(jnp.bfloat16)


def dot(a, b):
    return jnp.dot(a, b, preferred_element_type=jnp.float32)


def gather_kernel(row_slots, col_slots, strip, row_strips, col_strips,
                  fill_ref, ancestor, tiles, pick, rowq, starts_r, starts_c, sems):
    supers, fill = fill_ref.shape
    r, c = lax.axis_index("row"), lax.axis_index("col")
    mate = c + 1 - 2 * lax.rem(c, 2)
    slots = 2 * col_slots

    def one(k, carry):
        for s in range(2 * slots):
            pick[k, s] = 0
        for s in range(row_slots):
            starts_r[k, s] = 0
        for s in range(col_slots):
            starts_c[k, s] = 0
        values = [fill_ref[k, j] for j in range(fill)]
        for j in range(fill):
            s = values[j]
            in_row, in_col = s // row_strips, s // col_strips
            row_low, col_low = in_row * row_strips, in_col * col_strips
            row_slot, col_slot = jnp.int32(0), jnp.int32(0)
            for i in range(fill):
                if i != j:
                    less = values[i] < s
                    row_slot += jnp.where(less & (values[i] >= row_low), 1, 0)
                    col_slot += jnp.where(less & (values[i] >= col_low), 1, 0)
            rowq[k, j] = in_row * row_slots + row_slot

            @pl.when(in_row == r)
            def _():
                starts_r[k, row_slot] = s - row_low

            @pl.when(in_col == c)
            def _():
                starts_c[k, col_slot] = s - col_low
                pick[k, col_slot] = j
                pick[k, slots + col_slot] = 1

            @pl.when(in_col == mate)
            def _():
                pick[k, col_slots + col_slot] = j
                pick[k, slots + col_slots + col_slot] = 1

        for a in range(row_slots):
            for b in range(col_slots):
                copy_of(k, a, b).start()
        return carry

    def copy_of(k, a, b):
        row = pl.multiple_of(starts_r[k, a] * strip, strip)
        col = pl.multiple_of(starts_c[k, b] * strip, strip)
        return pltpu.make_async_copy(
            ancestor.at[pl.ds(row, strip), pl.ds(col, strip)],
            tiles.at[k, pl.ds(a * strip, strip), pl.ds(b * strip, strip)],
            sems.at[k, a, b],
        )

    lax.fori_loop(0, supers, one, 0)
    for k in range(supers):
        for a in range(row_slots):
            for b in range(col_slots):
                copy_of(k, a, b).wait()


def main_kernel(rows, cols, row_slots, col_slots,
                pick, rowq, tiles, panels, left, diag_inverse, upper, diag,
                own_tiles, mate_tiles, blocks, factor, factor_high, factor_low, product, by_row, dense, by_pair, final,
                terms, mate_terms, by_pair_diag, tile_sem,
                s_mate, r_mate, s_block, r_block, s_factor, r_factor, s_row, r_row, s_pair, r_pair, s_final, r_final,
                s_term, r_term, s_dpair, r_dpair, s_out, r_out):
    supers, _, strip, width = panels.shape
    waves = supers // 2
    pairs = cols // 2
    sub = strip // rows
    slots = 2 * col_slots
    diag_rows = diag_inverse.shape[1]
    chunk = diag_rows // pairs
    r, c = lax.axis_index("row"), lax.axis_index("col")
    core = lax.rem(c, 2)
    pair = c // 2
    mate = c + 1 - 2 * core
    sends = []

    def send(src, dst, ssem, rsem, row, col):
        copy = pltpu.make_async_remote_copy(
            src_ref=src, dst_ref=dst, send_sem=ssem, recv_sem=rsem, device_id=(row, col), device_id_type=MESH)
        copy.start()
        sends.append(copy)

    def arrive(dst, ssem, rsem):
        pltpu.make_async_remote_copy(
            src_ref=dst, dst_ref=dst, send_sem=ssem, recv_sem=rsem, device_id=(r, mate), device_id_type=MESH).wait_recv()

    def turn(value, step, size):
        return lax.rem(value + step, size)

    def rows_of(index, size):
        return pl.ds(pl.multiple_of(index * size, size), size)

    barrier = pltpu.get_barrier_semaphore()
    for d in range(1, cols):
        pl.semaphore_signal(barrier, inc=1, device_id=(r, turn(c, d, cols)), device_id_type=MESH)
    for d in range(1, rows):
        for col in (c, mate):
            pl.semaphore_signal(barrier, inc=1, device_id=(turn(r, d, rows), col), device_id_type=MESH)

    mine = rows_of(r, sub)
    own_copies = []
    for w in range(waves):
        copy = pltpu.make_async_copy(tiles.at[core * waves + w], own_tiles.at[w], tile_sem.at[w])
        copy.start()
        own_copies.append(copy)
    for w in range(waves):
        blocks[w][c] = panels[core * waves + w, 0, mine, :]

    pl.semaphore_wait(barrier, cols - 1 + 2 * (rows - 1))

    for w in range(waves):
        for d in range(1, cols):
            col = turn(c, d, cols)
            k = lax.rem(col, 2) * waves + w
            send(panels.at[k, 0, mine, :], blocks[w].at[c], s_block.at[w, d], r_block.at[w, c], r, col)
        send(tiles.at[(1 - core) * waves + w], mate_tiles.at[w], s_mate.at[w], r_mate.at[w], r, mate)

    for w in range(waves):
        k = core * waves + w
        for d in range(1, cols):
            source = turn(c, d, cols)
            arrive(blocks[w].at[source], s_block.at[w, d], r_block.at[w, source])
        for s in range(slots):
            factor[w, s, mine, :] = blocks[w][pick[k, s]] * pick[k, slots + s].astype(jnp.float32)
        for d in range(1, rows):
            part = factor.at[w, :, mine, :]
            send(part, part, s_factor.at[w, d], r_factor.at[w, r], turn(r, d, rows), c)

    half = col_slots * strip
    for w in range(waves):
        for d in range(1, rows):
            source = turn(r, d, rows)
            arrive(factor.at[w, :, rows_of(source, sub), :], s_factor.at[w, d], r_factor.at[w, source])
        for s in range(slots):
            high, low = split(factor[w, s])
            factor_high[pl.ds(s * strip, strip), :] = high
            factor_low[pl.ds(s * strip, strip), :] = low
        own_copies[w].wait()
        arrive(mate_tiles.at[w], s_mate.at[w], r_mate.at[w])

        def one(a, carry, w=w):
            band = rows_of(a, strip)
            total = None
            for first, held in ((0, own_tiles), (half, mate_tiles)):
                high, low = split(held[w, band, :])
                f_high = factor_high[pl.ds(first, half), :]
                f_low = factor_low[pl.ds(first, half), :]
                term = dot(high, f_low) + dot(low, f_high) + dot(high, f_high)
                total = term if total is None else total + term
            product[w, a] = total
            return carry

        lax.fori_loop(0, row_slots, one, 0)
        for d in range(1, rows):
            target = turn(r, d, rows)
            send(product.at[w, :, rows_of(target, sub), :], by_row[w].at[pl.ds(r * row_slots, row_slots)],
                 s_row.at[w, d], r_row.at[w, r], target, c)
        by_row[w][pl.ds(r * row_slots, row_slots)] = product[w, :, mine, :]

    for w in range(waves):
        k = core * waves + w
        for d in range(1, rows):
            source = turn(r, d, rows)
            arrive(by_row[w].at[pl.ds(source * row_slots, row_slots)], s_row.at[w, d], r_row.at[w, source])
        for j in range(cols):
            dense[w, j] = -by_row[w][rowq[k, j]]
        for d in range(1, pairs):
            target = turn(pair, d, pairs)
            send(dense.at[w, pl.ds(target * 2, 2)], by_pair.at[w, pair], s_pair.at[w, d], r_pair.at[w, pair],
                 r, target * 2 + core)
        by_pair[w, pair] = dense[w, pl.ds(pair * 2, 2)]

    for w in range(waves):
        k = core * waves + w
        for d in range(1, pairs):
            source = turn(pair, d, pairs)
            arrive(by_pair.at[w, source], s_pair.at[w, d], r_pair.at[w, source])
        total = by_pair[w, 0]
        for z in range(1, pairs):
            total += by_pair[w, z]
        final[w] = total
        for d in range(rows):
            target = turn(r, d, rows)
            for e in range(2):
                if d or e:
                    col = mate if e else c
                    send(final.at[w, lax.rem(col, 2)], upper.at[k, 0, mine, :],
                         s_final.at[w, d, e], r_final.at[w, r, core], target, col)
        upper[k, 0, mine, :] = final[w, core]

    for w in range(waves):
        for d in range(rows):
            source = turn(r, d, rows)
            for e in range(2):
                if d or e:
                    other = 1 - core if e else core
                    arrive(upper.at[other * waves + w, 0, rows_of(source, sub), :],
                           s_final.at[w, d, e], r_final.at[w, source, other])
        for e in range(2):
            k = e * waves + w
            l_high, l_low = split(left[k])
            u_high, u_low = split(upper[k, 0])
            terms[w, e] = dot(l_high, u_low) + dot(l_low, u_high) + dot(l_high, u_high)
        send(terms.at[w, 1 - core], mate_terms.at[w], s_term.at[w], r_term.at[w], r, mate)

    for w in range(waves):
        arrive(mate_terms.at[w], s_term.at[w], r_term.at[w])
        mate_terms[w] = mate_terms[w] + terms[w, core]
        for d in range(1, pairs):
            target = turn(pair, d, pairs)
            send(mate_terms.at[w, rows_of(target, chunk), :], by_pair_diag.at[w, pair],
                 s_dpair.at[w, d], r_dpair.at[w, pair], r, target * 2 + core)
        by_pair_diag[w, pair] = mate_terms[w, rows_of(pair, chunk), :]

    for w in range(waves):
        k = core * waves + w
        for d in range(1, pairs):
            source = turn(pair, d, pairs)
            arrive(by_pair_diag.at[w, source], s_dpair.at[w, d], r_dpair.at[w, source])
        total = by_pair_diag[w, 0]
        for z in range(1, pairs):
            total += by_pair_diag[w, z]
        place = rows_of(pair, chunk)
        diag[k, place, :] = diag_inverse[k, place, :] - total
        for d in range(1, cols):
            part = diag.at[k, place, :]
            send(part, part, s_out.at[w, d], r_out.at[w, c], r, turn(c, d, cols))

    for w in range(waves):
        for d in range(1, cols):
            source = turn(c, d, cols)
            k = lax.rem(source, 2) * waves + w
            arrive(diag.at[k, rows_of(source // 2, chunk), :], s_out.at[w, d], r_out.at[w, source])
    for copy in sends:
        copy.wait_send()


def local(ancestor, panels, diag_inverse, fill_strips):
    supers, local_fill, strip, width = panels.shape
    rows, cols = lax.axis_size("row"), lax.axis_size("col")
    fill = fill_strips.shape[1]
    row_slots = 2 * local_fill * cols // rows
    col_slots = 2 * local_fill
    row_strips, col_strips = ancestor.shape[0] // strip, ancestor.shape[1] // strip
    waves, pairs, sub, slots = supers // 2, cols // 2, strip // rows, 2 * col_slots
    diag_rows = diag_inverse.shape[1]
    chunk = diag_rows // pairs
    f32, i32, bf16 = jnp.float32, jnp.int32, jnp.bfloat16
    smem, vmem, anywhere = (pl.BlockSpec(memory_space=m) for m in (pltpu.SMEM, pltpu.VMEM, pl.ANY))
    dma = pltpu.SemaphoreType.DMA
    tiles, pick, rowq = pl.pallas_call(
        functools.partial(gather_kernel, row_slots, col_slots, strip, row_strips, col_strips),
        out_shape=(
            jax.ShapeDtypeStruct((supers, row_slots * strip, col_slots * strip), f32),
            jax.ShapeDtypeStruct((supers, 2 * slots), i32),
            jax.ShapeDtypeStruct((supers, fill), i32),
        ),
        in_specs=[smem, anywhere],
        out_specs=(anywhere, smem, smem),
        scratch_shapes=[
            pltpu.SMEM((supers, row_slots), i32),
            pltpu.SMEM((supers, col_slots), i32),
            dma((supers, row_slots, col_slots)),
        ],
        name="pick_tiles",
    )(fill_strips, ancestor)
    left = lax.dynamic_slice_in_dim(panels[:, 0], lax.axis_index("row") * diag_rows, diag_rows, 2)
    left = jnp.swapaxes(left, 1, 2)
    return pl.pallas_call(
        functools.partial(main_kernel, rows, cols, row_slots, col_slots),
        out_shape=(
            jax.ShapeDtypeStruct(panels.shape, f32),
            jax.ShapeDtypeStruct(diag_inverse.shape, f32),
        ),
        in_specs=[smem, smem, anywhere, vmem, vmem, vmem],
        out_specs=(vmem, vmem),
        scratch_shapes=[
            pltpu.VMEM((waves, row_slots * strip, col_slots * strip), f32),
            pltpu.VMEM((waves, row_slots * strip, col_slots * strip), f32),
            [pltpu.VMEM((cols, sub, width), f32)] * waves,
            pltpu.VMEM((waves, slots, strip, width), f32),
            pltpu.VMEM((slots * strip, width), bf16),
            pltpu.VMEM((slots * strip, width), bf16),
            pltpu.VMEM((waves, row_slots, strip, width), f32),
            [pltpu.VMEM((rows * row_slots, sub, width), f32)] * waves,
            pltpu.VMEM((waves, cols, sub, width), f32),
            pltpu.VMEM((waves, pairs, 2, sub, width), f32),
            pltpu.VMEM((waves, 2, sub, width), f32),
            pltpu.VMEM((waves, 2, diag_rows, width), f32),
            pltpu.VMEM((waves, diag_rows, width), f32),
            pltpu.VMEM((waves, pairs, chunk, width), f32),
            dma((waves,)),
            dma((waves,)), dma((waves,)),
            dma((waves, cols)), dma((waves, cols)),
            dma((waves, rows)), dma((waves, rows)),
            dma((waves, rows)), dma((waves, rows)),
            dma((waves, pairs)), dma((waves, pairs)),
            dma((waves, rows, 2)), dma((waves, rows, 2)),
            dma((waves,)), dma((waves,)),
            dma((waves, pairs)), dma((waves, pairs)),
            dma((waves, cols)), dma((waves, cols)),
        ],
        compiler_params=pltpu.CompilerParams(
            collective_id=0, has_side_effects=True, vmem_limit_bytes=56 * 2**20),
        name="update",
    )(pick, rowq, tiles, panels, left, diag_inverse)


def solution(mesh):
    return jax.shard_map(
        local,
        mesh=mesh,
        in_specs=(P("row", "col"), P(None, "col", None, None), P(None, "row", None), P()),
        out_specs=(P(None, "col", None, None), P(None, "row", None)),
        check_vma=False,
    )
```

```python
import functools

import jax
import jax.numpy as jnp
from jax import lax
from jax.experimental import pallas as pl
from jax.experimental.pallas import tpu as pltpu
from jax.sharding import PartitionSpec as P

MESH = pl.DeviceIdType.MESH


def split(x):
    high = x.astype(jnp.bfloat16)
    return high, (x - high.astype(jnp.float32)).astype(jnp.bfloat16)


def dot(a, b):
    return jnp.dot(a, b, preferred_element_type=jnp.float32)


def dot_left(a, b):
    return lax.dot_general(a, b, (((0,), (0,)), ((), ())), preferred_element_type=jnp.float32)


def gather_kernel(row_slots, col_slots, strip, row_strips, col_strips,
                  fill_ref, ancestor, tiles, pick, rowq, starts_r, starts_c, sems):
    supers, fill = fill_ref.shape
    r, c = lax.axis_index("row"), lax.axis_index("col")
    mate = c + 1 - 2 * lax.rem(c, 2)
    slots = 2 * col_slots

    def one(k, carry):
        for s in range(2 * slots):
            pick[k, s] = 0
        for s in range(row_slots):
            starts_r[k, s] = 0
        for s in range(col_slots):
            starts_c[k, s] = 0
        values = [fill_ref[k, j] for j in range(fill)]
        for j in range(fill):
            s = values[j]
            in_row, in_col = s // row_strips, s // col_strips
            row_low, col_low = in_row * row_strips, in_col * col_strips
            row_slot, col_slot = jnp.int32(0), jnp.int32(0)
            for i in range(fill):
                if i != j:
                    less = values[i] < s
                    row_slot += jnp.where(less & (values[i] >= row_low), 1, 0)
                    col_slot += jnp.where(less & (values[i] >= col_low), 1, 0)
            rowq[k, j] = in_row * row_slots + row_slot

            @pl.when(in_row == r)
            def _():
                starts_r[k, row_slot] = s - row_low

            @pl.when(in_col == c)
            def _():
                starts_c[k, col_slot] = s - col_low
                pick[k, col_slot] = j
                pick[k, slots + col_slot] = 1

            @pl.when(in_col == mate)
            def _():
                pick[k, col_slots + col_slot] = j
                pick[k, slots + col_slots + col_slot] = 1

        for a in range(row_slots):
            for b in range(col_slots):
                copy_of(k, a, b).start()
        return carry

    def copy_of(k, a, b):
        row = pl.multiple_of(starts_r[k, a] * strip, strip)
        col = pl.multiple_of(starts_c[k, b] * strip, strip)
        return pltpu.make_async_copy(
            ancestor.at[pl.ds(row, strip), pl.ds(col, strip)],
            tiles.at[k, pl.ds(a * strip, strip), pl.ds(b * strip, strip)],
            sems.at[k, a, b],
        )

    lax.fori_loop(0, supers, one, 0)
    for k in range(supers):
        for a in range(row_slots):
            for b in range(col_slots):
                copy_of(k, a, b).wait()


def main_kernel(rows, cols, halves, row_slots, col_slots,
                pick, rowq, tiles, panels, left, diag_inverse, upper, diag,
                own_tiles, mate_tiles, blocks, factor, factor_high, factor_low, product, by_row, dense, by_pair, final,
                terms, mate_terms, by_pair_diag, tile_sem,
                s_mate, r_mate, s_block, r_block, s_factor, r_factor, s_row, r_row, s_pair, r_pair, s_final, r_final,
                s_term, r_term, s_dpair, r_dpair, s_out, r_out, s_last, r_last):
    supers, _, strip, width = panels.shape
    held = supers // 2
    waves = held * halves
    part = width // halves
    pairs = cols // 2
    sub = strip // rows
    slots = 2 * col_slots
    diag_rows = diag_inverse.shape[1]
    chunk = diag_rows // pairs
    r, c = lax.axis_index("row"), lax.axis_index("col")
    core = lax.rem(c, 2)
    pair = c // 2
    mate = c + 1 - 2 * core
    sends = []

    def send(src, dst, ssem, rsem, row, col):
        copy = pltpu.make_async_remote_copy(
            src_ref=src, dst_ref=dst, send_sem=ssem, recv_sem=rsem, device_id=(row, col), device_id_type=MESH)
        copy.start()
        sends.append(copy)

    def arrive(dst, ssem, rsem):
        pltpu.make_async_remote_copy(
            src_ref=dst, dst_ref=dst, send_sem=ssem, recv_sem=rsem, device_id=(r, mate), device_id_type=MESH).wait_recv()

    def turn(value, step, size):
        return lax.rem(value + step, size)

    def rows_of(index, size):
        return pl.ds(pl.multiple_of(index * size, size), size)

    def which(w, of_core):
        return of_core * held + w // halves, pl.ds((w % halves) * part, part)

    barrier = pltpu.get_barrier_semaphore()
    for d in range(1, cols):
        pl.semaphore_signal(barrier, inc=1, device_id=(r, turn(c, d, cols)), device_id_type=MESH)
    for d in range(1, rows):
        for col in (c, mate):
            pl.semaphore_signal(barrier, inc=1, device_id=(turn(r, d, rows), col), device_id_type=MESH)

    mine = rows_of(r, sub)
    own_copies = []
    for i in range(held):
        copy = pltpu.make_async_copy(tiles.at[core * held + i], own_tiles.at[i], tile_sem.at[i])
        copy.start()
        own_copies.append(copy)
    for w in range(waves):
        k, lanes = which(w, core)
        blocks[w][c] = panels[k, 0, mine, lanes]

    pl.semaphore_wait(barrier, cols - 1 + 2 * (rows - 1))

    for w in range(waves):
        for d in range(1, cols):
            col = turn(c, d, cols)
            k, lanes = which(w, lax.rem(col, 2))
            send(panels.at[k, 0, mine, lanes], blocks[w].at[c], s_block.at[w, d], r_block.at[w, c], r, col)
        if w % halves == 0:
            i = w // halves
            send(tiles.at[(1 - core) * held + i], mate_tiles.at[i], s_mate.at[i], r_mate.at[i], r, mate)

    def select(w):
        k, _ = which(w, core)
        for d in range(1, cols):
            source = turn(c, d, cols)
            arrive(blocks[w].at[source], s_block.at[w, d], r_block.at[w, source])
        for s in range(slots):
            factor[w, s, mine, :] = blocks[w][pick[k, s]] * pick[k, slots + s].astype(jnp.float32)
        for d in range(1, rows):
            share = factor.at[w, :, mine, :]
            send(share, share, s_factor.at[w, d], r_factor.at[w, r], turn(r, d, rows), c)

    half = col_slots * strip

    def multiply(w):
        i = w // halves
        for d in range(1, rows):
            source = turn(r, d, rows)
            arrive(factor.at[w, :, rows_of(source, sub), :], s_factor.at[w, d], r_factor.at[w, source])
        for s in range(slots):
            high, low = split(factor[w, s])
            factor_high[pl.ds(s * strip, strip), :] = high
            factor_low[pl.ds(s * strip, strip), :] = low
        if w % halves == 0:
            own_copies[i].wait()
            arrive(mate_tiles.at[i], s_mate.at[i], r_mate.at[i])

        def one(a, carry):
            band = rows_of(a, strip)
            total = None
            for first, source in ((0, own_tiles), (half, mate_tiles)):
                high, low = split(source[i, band, :])
                f_high = factor_high[pl.ds(first, half), :]
                f_low = factor_low[pl.ds(first, half), :]
                term = dot(high, f_low) + dot(low, f_high) + dot(high, f_high)
                total = term if total is None else total + term
            product[w, a] = total
            return carry

        lax.fori_loop(0, row_slots, one, 0)
        for d in range(1, rows):
            target = turn(r, d, rows)
            send(product.at[w, :, rows_of(target, sub), :], by_row[w].at[pl.ds(r * row_slots, row_slots)],
                 s_row.at[w, d], r_row.at[w, r], target, c)
        by_row[w][pl.ds(r * row_slots, row_slots)] = product[w, :, mine, :]

    def scatter(w):
        k, _ = which(w, core)
        for d in range(1, rows):
            source = turn(r, d, rows)
            arrive(by_row[w].at[pl.ds(source * row_slots, row_slots)], s_row.at[w, d], r_row.at[w, source])
        for j in range(cols):
            dense[w, j] = -by_row[w][rowq[k, j]]
        for d in range(1, pairs):
            target = turn(pair, d, pairs)
            send(dense.at[w, pl.ds(target * 2, 2)], by_pair.at[w, pair], s_pair.at[w, d], r_pair.at[w, pair],
                 r, target * 2 + core)
        by_pair[w, pair] = dense[w, pl.ds(pair * 2, 2)]

    def spread(w):
        k, lanes = which(w, core)
        for d in range(1, pairs):
            source = turn(pair, d, pairs)
            arrive(by_pair.at[w, source], s_pair.at[w, d], r_pair.at[w, source])
        total = by_pair[w, 0]
        for z in range(1, pairs):
            total += by_pair[w, z]
        final[w] = total
        for d in range(rows):
            target = turn(r, d, rows)
            for e in range(2):
                if d or e:
                    col = mate if e else c
                    send(final.at[w, lax.rem(col, 2)], upper.at[k, 0, mine, lanes],
                         s_final.at[w, d, e], r_final.at[w, r, core], target, col)
        upper[k, 0, mine, lanes] = final[w, core]

    def term_of(w):
        for d in range(rows):
            source = turn(r, d, rows)
            for e in range(2):
                if d or e:
                    other = 1 - core if e else core
                    k, lanes = which(w, other)
                    arrive(upper.at[k, 0, rows_of(source, sub), lanes],
                           s_final.at[w, d, e], r_final.at[w, source, other])
        for e in range(2):
            k, lanes = which(w, e)
            l_high, l_low = split(left[k])
            u_high, u_low = split(upper[k, 0, :, lanes])
            terms[w, e] = dot_left(l_high, u_low) + dot_left(l_low, u_high) + dot_left(l_high, u_high)
        send(terms.at[w, 1 - core], mate_terms.at[w], s_term.at[w], r_term.at[w], r, mate)

    def term_scatter(w):
        arrive(mate_terms.at[w], s_term.at[w], r_term.at[w])
        mate_terms[w] = mate_terms[w] + terms[w, core]
        for d in range(1, pairs):
            target = turn(pair, d, pairs)
            send(mate_terms.at[w, rows_of(target, chunk), :], by_pair_diag.at[w, pair],
                 s_dpair.at[w, d], r_dpair.at[w, pair], r, target * 2 + core)
        by_pair_diag[w, pair] = mate_terms[w, rows_of(pair, chunk), :]

    def term_spread(w):
        k, lanes = which(w, core)
        for d in range(1, pairs):
            source = turn(pair, d, pairs)
            arrive(by_pair_diag.at[w, source], s_dpair.at[w, d], r_dpair.at[w, source])
        total = by_pair_diag[w, 0]
        for z in range(1, pairs):
            total += by_pair_diag[w, z]
        place = rows_of(pair, chunk)
        diag[k, place, lanes] = diag_inverse[k, place, lanes] - total
        share = diag.at[k, place, lanes]
        for d in range(1, pairs):
            send(share, share, s_out.at[w, d], r_out.at[w, pair], r, turn(pair, d, pairs) * 2 + core)

    def hand_over(w):
        k, lanes = which(w, core)
        for d in range(1, pairs):
            source = turn(pair, d, pairs)
            arrive(diag.at[k, rows_of(source, chunk), lanes], s_out.at[w, d], r_out.at[w, source])
        share = diag.at[k, :, lanes]
        send(share, share, s_last.at[w], r_last.at[w], r, mate)

    def last(w):
        k, lanes = which(w, 1 - core)
        arrive(diag.at[k, :, lanes], s_last.at[w], r_last.at[w])

    stages = (select, multiply, scatter, spread, term_of, term_scatter, term_spread, hand_over, last)
    for step in range(waves + len(stages) - 1):
        for index in reversed(range(len(stages))):
            if 0 <= step - index < waves:
                stages[index](step - index)
    for copy in sends:
        copy.wait_send()


def local(ancestor, panels, diag_inverse, fill_strips):
    supers, local_fill, strip, width = panels.shape
    rows, cols = lax.axis_size("row"), lax.axis_size("col")
    fill = fill_strips.shape[1]
    row_slots = 2 * local_fill * cols // rows
    col_slots = 2 * local_fill
    row_strips, col_strips = ancestor.shape[0] // strip, ancestor.shape[1] // strip
    halves = 2 if width % 256 == 0 else 1
    held, part = supers // 2, width // halves
    waves, pairs, sub, slots = held * halves, cols // 2, strip // rows, 2 * col_slots
    diag_rows = diag_inverse.shape[1]
    chunk = diag_rows // pairs
    f32, i32, bf16 = jnp.float32, jnp.int32, jnp.bfloat16
    smem, vmem, anywhere = (pl.BlockSpec(memory_space=m) for m in (pltpu.SMEM, pltpu.VMEM, pl.ANY))
    dma = pltpu.SemaphoreType.DMA
    tiles, pick, rowq = pl.pallas_call(
        functools.partial(gather_kernel, row_slots, col_slots, strip, row_strips, col_strips),
        out_shape=(
            jax.ShapeDtypeStruct((supers, row_slots * strip, col_slots * strip), f32),
            jax.ShapeDtypeStruct((supers, 2 * slots), i32),
            jax.ShapeDtypeStruct((supers, fill), i32),
        ),
        in_specs=[smem, anywhere],
        out_specs=(vmem, smem, smem),
        scratch_shapes=[
            pltpu.SMEM((supers, row_slots), i32),
            pltpu.SMEM((supers, col_slots), i32),
            dma((supers, row_slots, col_slots)),
        ],
        compiler_params=pltpu.CompilerParams(vmem_limit_bytes=56 * 2**20),
        name="pick_tiles",
    )(fill_strips, ancestor)
    left = lax.dynamic_slice_in_dim(panels[:, 0], lax.axis_index("row") * diag_rows, diag_rows, 2)
    return pl.pallas_call(
        functools.partial(main_kernel, rows, cols, halves, row_slots, col_slots),
        out_shape=(
            jax.ShapeDtypeStruct(panels.shape, f32),
            jax.ShapeDtypeStruct(diag_inverse.shape, f32),
        ),
        in_specs=[smem, smem, anywhere, vmem, vmem, vmem],
        out_specs=(vmem, vmem),
        scratch_shapes=[
            pltpu.VMEM((held, row_slots * strip, col_slots * strip), f32),
            pltpu.VMEM((held, row_slots * strip, col_slots * strip), f32),
            [pltpu.VMEM((cols, sub, part), f32)] * waves,
            pltpu.VMEM((waves, slots, strip, part), f32),
            pltpu.VMEM((slots * strip, part), bf16),
            pltpu.VMEM((slots * strip, part), bf16),
            pltpu.VMEM((waves, row_slots, strip, part), f32),
            [pltpu.VMEM((rows * row_slots, sub, part), f32)] * waves,
            pltpu.VMEM((waves, cols, sub, part), f32),
            pltpu.VMEM((waves, pairs, 2, sub, part), f32),
            pltpu.VMEM((waves, 2, sub, part), f32),
            pltpu.VMEM((waves, 2, diag_rows, part), f32),
            pltpu.VMEM((waves, diag_rows, part), f32),
            pltpu.VMEM((waves, pairs, chunk, part), f32),
            dma((held,)),
            dma((held,)), dma((held,)),
            dma((waves, cols)), dma((waves, cols)),
            dma((waves, rows)), dma((waves, rows)),
            dma((waves, rows)), dma((waves, rows)),
            dma((waves, pairs)), dma((waves, pairs)),
            dma((waves, rows, 2)), dma((waves, rows, 2)),
            dma((waves,)), dma((waves,)),
            dma((waves, pairs)), dma((waves, pairs)),
            dma((waves, pairs)), dma((waves, pairs)),
            dma((waves,)), dma((waves,)),
        ],
        compiler_params=pltpu.CompilerParams(
            collective_id=0, has_side_effects=True, vmem_limit_bytes=56 * 2**20),
        name="update",
    )(pick, rowq, tiles, panels, left, diag_inverse)


def solution(mesh):
    return jax.shard_map(
        local,
        mesh=mesh,
        in_specs=(P("row", "col"), P(None, "col", None, None), P(None, "row", None), P()),
        out_specs=(P(None, "col", None, None), P(None, "row", None)),
        check_vma=False,
    )
```

```python
import functools

import jax
import jax.numpy as jnp
from jax import lax
from jax.experimental import pallas as pl
from jax.experimental.pallas import tpu as pltpu
from jax.sharding import PartitionSpec as P

MESH = pl.DeviceIdType.MESH


def split(x):
    high = x.astype(jnp.bfloat16)
    return high, (x - high.astype(jnp.float32)).astype(jnp.bfloat16)


def dot(a, b):
    return jnp.dot(a, b, preferred_element_type=jnp.float32)


def dot_left(a, b):
    return lax.dot_general(a, b, (((0,), (0,)), ((), ())), preferred_element_type=jnp.float32)


def gather_kernel(row_slots, col_slots, strip, row_strips, col_strips,
                  fill_ref, ancestor, tiles, pick, rowq, starts_r, starts_c, sems):
    supers, fill = fill_ref.shape
    r, c = lax.axis_index("row"), lax.axis_index("col")
    mate = c + 1 - 2 * lax.rem(c, 2)
    slots = 2 * col_slots

    def one(k, carry):
        for s in range(2 * slots):
            pick[k, s] = 0
        for s in range(row_slots):
            starts_r[k, s] = 0
        for s in range(col_slots):
            starts_c[k, s] = 0
        values = [fill_ref[k, j] for j in range(fill)]
        for j in range(fill):
            s = values[j]
            in_row, in_col = s // row_strips, s // col_strips
            row_low, col_low = in_row * row_strips, in_col * col_strips
            row_slot, col_slot = jnp.int32(0), jnp.int32(0)
            for i in range(fill):
                if i != j:
                    less = values[i] < s
                    row_slot += jnp.where(less & (values[i] >= row_low), 1, 0)
                    col_slot += jnp.where(less & (values[i] >= col_low), 1, 0)
            rowq[k, j] = in_row * row_slots + row_slot

            @pl.when(in_row == r)
            def _():
                starts_r[k, row_slot] = s - row_low

            @pl.when(in_col == c)
            def _():
                starts_c[k, col_slot] = s - col_low
                pick[k, col_slot] = j
                pick[k, slots + col_slot] = 1

            @pl.when(in_col == mate)
            def _():
                pick[k, col_slots + col_slot] = j
                pick[k, slots + col_slots + col_slot] = 1

        for a in range(row_slots):
            for b in range(col_slots):
                copy_of(k, a, b).start()
        return carry

    def copy_of(k, a, b):
        row = pl.multiple_of(starts_r[k, a] * strip, strip)
        col = pl.multiple_of(starts_c[k, b] * strip, strip)
        return pltpu.make_async_copy(
            ancestor.at[pl.ds(row, strip), pl.ds(col, strip)],
            tiles.at[k, pl.ds(a * strip, strip), pl.ds(b * strip, strip)],
            sems.at[k, a, b],
        )

    lax.fori_loop(0, supers, one, 0)
    for k in range(supers):
        for a in range(row_slots):
            for b in range(col_slots):
                copy_of(k, a, b).wait()


def main_kernel(rows, cols, halves, row_slots, col_slots,
                pick, rowq, tiles, panels, left, diag_inverse, upper, diag,
                own_tiles, mate_tiles, blocks, factor, factor_both, product, by_row, dense, by_pair, final,
                terms, mate_terms, by_pair_diag, tile_sem,
                s_mate, r_mate, s_block, r_block, s_factor, r_factor, s_row, r_row, s_pair, r_pair, s_final, r_final,
                s_term, r_term, s_dpair, r_dpair, s_out, r_out, s_last, r_last):
    supers, _, strip, width = panels.shape
    held = supers // 2
    waves = held * halves
    part = width // halves
    pairs = cols // 2
    sub = strip // rows
    slots = 2 * col_slots
    diag_rows = diag_inverse.shape[1]
    chunk = diag_rows // pairs
    r, c = lax.axis_index("row"), lax.axis_index("col")
    core = lax.rem(c, 2)
    pair = c // 2
    mate = c + 1 - 2 * core
    sends = []

    def send(src, dst, ssem, rsem, row, col):
        copy = pltpu.make_async_remote_copy(
            src_ref=src, dst_ref=dst, send_sem=ssem, recv_sem=rsem, device_id=(row, col), device_id_type=MESH)
        copy.start()
        sends.append(copy)

    def arrive(dst, ssem, rsem):
        pltpu.make_async_remote_copy(
            src_ref=dst, dst_ref=dst, send_sem=ssem, recv_sem=rsem, device_id=(r, mate), device_id_type=MESH).wait_recv()

    def turn(value, step, size):
        return lax.rem(value + step, size)

    def rows_of(index, size):
        return pl.ds(pl.multiple_of(index * size, size), size)

    def which(w, of_core):
        return of_core * held + w // halves, pl.ds((w % halves) * part, part)

    barrier = pltpu.get_barrier_semaphore()
    for d in range(1, cols):
        pl.semaphore_signal(barrier, inc=1, device_id=(r, turn(c, d, cols)), device_id_type=MESH)
    for d in range(1, rows):
        for col in (c, mate):
            pl.semaphore_signal(barrier, inc=1, device_id=(turn(r, d, rows), col), device_id_type=MESH)

    mine = rows_of(r, sub)
    own_copies = []
    for i in range(held):
        copy = pltpu.make_async_copy(tiles.at[core * held + i], own_tiles.at[i], tile_sem.at[i])
        copy.start()
        own_copies.append(copy)
    for w in range(waves):
        k, lanes = which(w, core)
        blocks[w][c] = panels[k, 0, mine, lanes]

    pl.semaphore_wait(barrier, cols - 1 + 2 * (rows - 1))

    for w in range(waves):
        for d in range(1, cols):
            col = turn(c, d, cols)
            k, lanes = which(w, lax.rem(col, 2))
            send(panels.at[k, 0, mine, lanes], blocks[w].at[c], s_block.at[w, d], r_block.at[w, c], r, col)
        if w % halves == 0:
            i = w // halves
            send(tiles.at[(1 - core) * held + i], mate_tiles.at[i], s_mate.at[i], r_mate.at[i], r, mate)

    def select(w):
        k, _ = which(w, core)
        for d in range(1, cols):
            source = turn(c, d, cols)
            arrive(blocks[w].at[source], s_block.at[w, d], r_block.at[w, source])
        for s in range(slots):
            factor[w, s, mine, :] = blocks[w][pick[k, s]] * pick[k, slots + s].astype(jnp.float32)
        for d in range(1, rows):
            share = factor.at[w, :, mine, :]
            send(share, share, s_factor.at[w, d], r_factor.at[w, r], turn(r, d, rows), c)

    half = col_slots * strip

    def multiply(w):
        i = w // halves
        for d in range(1, rows):
            source = turn(r, d, rows)
            arrive(factor.at[w, :, rows_of(source, sub), :], s_factor.at[w, d], r_factor.at[w, source])
        for s in range(slots):
            high, low = split(factor[w, s])
            factor_both[pl.ds(s * strip, strip), pl.ds(0, part)] = high
            factor_both[pl.ds(s * strip, strip), pl.ds(part, part)] = low
        if w % halves == 0:
            own_copies[i].wait()
            arrive(mate_tiles.at[i], s_mate.at[i], r_mate.at[i])

        def one(a, carry):
            band = rows_of(a, strip)
            total = None
            for first, source in ((0, own_tiles), (half, mate_tiles)):
                high, low = split(source[i, band, :])
                both = dot(high, factor_both[pl.ds(first, half), :])
                term = both[:, part:] + dot(low, factor_both[pl.ds(first, half), pl.ds(0, part)]) + both[:, :part]
                total = term if total is None else total + term
            product[w, a] = total
            return carry

        lax.fori_loop(0, row_slots, one, 0)
        for d in range(1, rows):
            target = turn(r, d, rows)
            send(product.at[w, :, rows_of(target, sub), :], by_row[w].at[pl.ds(r * row_slots, row_slots)],
                 s_row.at[w, d], r_row.at[w, r], target, c)
        by_row[w][pl.ds(r * row_slots, row_slots)] = product[w, :, mine, :]

    def scatter(w):
        k, _ = which(w, core)
        for d in range(1, rows):
            source = turn(r, d, rows)
            arrive(by_row[w].at[pl.ds(source * row_slots, row_slots)], s_row.at[w, d], r_row.at[w, source])
        for j in range(cols):
            dense[w, j] = -by_row[w][rowq[k, j]]
        for d in range(1, pairs):
            target = turn(pair, d, pairs)
            send(dense.at[w, pl.ds(target * 2, 2)], by_pair.at[w, pair], s_pair.at[w, d], r_pair.at[w, pair],
                 r, target * 2 + core)
        by_pair[w, pair] = dense[w, pl.ds(pair * 2, 2)]

    def spread(w):
        k, lanes = which(w, core)
        for d in range(1, pairs):
            source = turn(pair, d, pairs)
            arrive(by_pair.at[w, source], s_pair.at[w, d], r_pair.at[w, source])
        total = by_pair[w, 0]
        for z in range(1, pairs):
            total += by_pair[w, z]
        final[w] = total
        for d in range(rows):
            target = turn(r, d, rows)
            for e in range(2):
                if d or e:
                    col = mate if e else c
                    send(final.at[w, lax.rem(col, 2)], upper.at[k, 0, mine, lanes],
                         s_final.at[w, d, e], r_final.at[w, r, core], target, col)
        upper[k, 0, mine, lanes] = final[w, core]

    def term_of(w):
        for d in range(rows):
            source = turn(r, d, rows)
            for e in range(2):
                if d or e:
                    other = 1 - core if e else core
                    k, lanes = which(w, other)
                    arrive(upper.at[k, 0, rows_of(source, sub), lanes],
                           s_final.at[w, d, e], r_final.at[w, source, other])
        for e in range(2):
            k, lanes = which(w, e)
            l_high, l_low = split(left[k])
            u_high, u_low = split(upper[k, 0, :, lanes])
            terms[w, e] = dot_left(l_high, u_low) + dot_left(l_low, u_high) + dot_left(l_high, u_high)
        send(terms.at[w, 1 - core], mate_terms.at[w], s_term.at[w], r_term.at[w], r, mate)

    def term_scatter(w):
        arrive(mate_terms.at[w], s_term.at[w], r_term.at[w])
        mate_terms[w] = mate_terms[w] + terms[w, core]
        for d in range(1, pairs):
            target = turn(pair, d, pairs)
            send(mate_terms.at[w, rows_of(target, chunk), :], by_pair_diag.at[w, pair],
                 s_dpair.at[w, d], r_dpair.at[w, pair], r, target * 2 + core)
        by_pair_diag[w, pair] = mate_terms[w, rows_of(pair, chunk), :]

    def term_spread(w):
        k, lanes = which(w, core)
        for d in range(1, pairs):
            source = turn(pair, d, pairs)
            arrive(by_pair_diag.at[w, source], s_dpair.at[w, d], r_dpair.at[w, source])
        total = by_pair_diag[w, 0]
        for z in range(1, pairs):
            total += by_pair_diag[w, z]
        place = rows_of(pair, chunk)
        diag[k, place, lanes] = diag_inverse[k, place, lanes] - total
        share = diag.at[k, place, lanes]
        for d in range(1, pairs):
            send(share, share, s_out.at[w, d], r_out.at[w, pair], r, turn(pair, d, pairs) * 2 + core)

    def hand_over(w):
        k, lanes = which(w, core)
        for d in range(1, pairs):
            source = turn(pair, d, pairs)
            arrive(diag.at[k, rows_of(source, chunk), lanes], s_out.at[w, d], r_out.at[w, source])
        share = diag.at[k, :, lanes]
        send(share, share, s_last.at[w], r_last.at[w], r, mate)

    def last(w):
        k, lanes = which(w, 1 - core)
        arrive(diag.at[k, :, lanes], s_last.at[w], r_last.at[w])

    stages = ((select, 0, 52), (multiply, 32, 96), (scatter, 75, 141), (spread, 125, 167), (term_of, 156, 186),
              (term_scatter, 166, 193), (term_spread, 174, 213), (hand_over, 192, 241), (last, 264, 293))
    order = [
        (first + (end - first) * w / max(1, waves - 1), stage, w) for stage, first, end in stages for w in range(waves)
    ]
    for _, stage, w in sorted(order, key=lambda item: item[0]):
        stage(w)
    for copy in sends:
        copy.wait_send()


def local(ancestor, panels, diag_inverse, fill_strips):
    supers, local_fill, strip, width = panels.shape
    rows, cols = lax.axis_size("row"), lax.axis_size("col")
    fill = fill_strips.shape[1]
    row_slots = 2 * local_fill * cols // rows
    col_slots = 2 * local_fill
    row_strips, col_strips = ancestor.shape[0] // strip, ancestor.shape[1] // strip
    halves = max(1, width // 128)
    held, part = supers // 2, width // halves
    waves, pairs, sub, slots = held * halves, cols // 2, strip // rows, 2 * col_slots
    diag_rows = diag_inverse.shape[1]
    chunk = diag_rows // pairs
    f32, i32, bf16 = jnp.float32, jnp.int32, jnp.bfloat16
    smem, vmem, anywhere = (pl.BlockSpec(memory_space=m) for m in (pltpu.SMEM, pltpu.VMEM, pl.ANY))
    dma = pltpu.SemaphoreType.DMA
    tiles, pick, rowq = pl.pallas_call(
        functools.partial(gather_kernel, row_slots, col_slots, strip, row_strips, col_strips),
        out_shape=(
            jax.ShapeDtypeStruct((supers, row_slots * strip, col_slots * strip), f32),
            jax.ShapeDtypeStruct((supers, 2 * slots), i32),
            jax.ShapeDtypeStruct((supers, fill), i32),
        ),
        in_specs=[smem, anywhere],
        out_specs=(vmem, smem, smem),
        scratch_shapes=[
            pltpu.SMEM((supers, row_slots), i32),
            pltpu.SMEM((supers, col_slots), i32),
            dma((supers, row_slots, col_slots)),
        ],
        compiler_params=pltpu.CompilerParams(vmem_limit_bytes=56 * 2**20),
        name="pick_tiles",
    )(fill_strips, ancestor)
    left = lax.dynamic_slice_in_dim(panels[:, 0], lax.axis_index("row") * diag_rows, diag_rows, 2)
    return pl.pallas_call(
        functools.partial(main_kernel, rows, cols, halves, row_slots, col_slots),
        out_shape=(
            jax.ShapeDtypeStruct(panels.shape, f32),
            jax.ShapeDtypeStruct(diag_inverse.shape, f32),
        ),
        in_specs=[smem, smem, anywhere, vmem, vmem, vmem],
        out_specs=(vmem, vmem),
        scratch_shapes=[
            pltpu.VMEM((held, row_slots * strip, col_slots * strip), f32),
            pltpu.VMEM((held, row_slots * strip, col_slots * strip), f32),
            [pltpu.VMEM((cols, sub, part), f32)] * waves,
            pltpu.VMEM((waves, slots, strip, part), f32),
            pltpu.VMEM((slots * strip, 2 * part), bf16),
            pltpu.VMEM((waves, row_slots, strip, part), f32),
            [pltpu.VMEM((rows * row_slots, sub, part), f32)] * waves,
            pltpu.VMEM((waves, cols, sub, part), f32),
            pltpu.VMEM((waves, pairs, 2, sub, part), f32),
            pltpu.VMEM((waves, 2, sub, part), f32),
            pltpu.VMEM((waves, 2, diag_rows, part), f32),
            pltpu.VMEM((waves, diag_rows, part), f32),
            pltpu.VMEM((waves, pairs, chunk, part), f32),
            dma((held,)),
            dma((held,)), dma((held,)),
            dma((waves, cols)), dma((waves, cols)),
            dma((waves, rows)), dma((waves, rows)),
            dma((waves, rows)), dma((waves, rows)),
            dma((waves, pairs)), dma((waves, pairs)),
            dma((waves, rows, 2)), dma((waves, rows, 2)),
            dma((waves,)), dma((waves,)),
            dma((waves, pairs)), dma((waves, pairs)),
            dma((waves, pairs)), dma((waves, pairs)),
            dma((waves,)), dma((waves,)),
        ],
        compiler_params=pltpu.CompilerParams(
            collective_id=0, has_side_effects=True, vmem_limit_bytes=56 * 2**20),
        name="update",
    )(pick, rowq, tiles, panels, left, diag_inverse)


def solution(mesh):
    return jax.shard_map(
        local,
        mesh=mesh,
        in_specs=(P("row", "col"), P(None, "col", None, None), P(None, "row", None), P()),
        out_specs=(P(None, "col", None, None), P(None, "row", None)),
        check_vma=False,
    )
```

```python
import functools

import jax
import jax.numpy as jnp
from jax import lax
from jax.experimental import pallas as pl
from jax.experimental.pallas import tpu as pltpu
from jax.sharding import PartitionSpec as P

MESH = pl.DeviceIdType.MESH


def split(x):
    high = x.astype(jnp.bfloat16)
    return high, (x - high.astype(jnp.float32)).astype(jnp.bfloat16)


def dot(a, b):
    return jnp.dot(a, b, preferred_element_type=jnp.float32)


def dot_left(a, b):
    return lax.dot_general(a, b, (((0,), (0,)), ((), ())), preferred_element_type=jnp.float32)


def gather_kernel(row_slots, col_slots, strip, row_strips, col_strips,
                  fill_ref, ancestor, tiles, pick, rowq, starts_r, starts_c, sems):
    supers, fill = fill_ref.shape
    r, c = lax.axis_index("row"), lax.axis_index("col")
    mate = c + 1 - 2 * lax.rem(c, 2)
    slots = 2 * col_slots

    def one(k, carry):
        for s in range(2 * slots):
            pick[k, s] = 0
        for s in range(row_slots):
            starts_r[k, s] = 0
        for s in range(col_slots):
            starts_c[k, s] = 0
        values = [fill_ref[k, j] for j in range(fill)]
        for j in range(fill):
            s = values[j]
            in_row, in_col = s // row_strips, s // col_strips
            row_low, col_low = in_row * row_strips, in_col * col_strips
            row_slot, col_slot = jnp.int32(0), jnp.int32(0)
            for i in range(fill):
                if i != j:
                    less = values[i] < s
                    row_slot += jnp.where(less & (values[i] >= row_low), 1, 0)
                    col_slot += jnp.where(less & (values[i] >= col_low), 1, 0)
            rowq[k, j] = in_row * row_slots + row_slot

            @pl.when(in_row == r)
            def _():
                starts_r[k, row_slot] = s - row_low

            @pl.when(in_col == c)
            def _():
                starts_c[k, col_slot] = s - col_low
                pick[k, col_slot] = j
                pick[k, slots + col_slot] = 1

            @pl.when(in_col == mate)
            def _():
                pick[k, col_slots + col_slot] = j
                pick[k, slots + col_slots + col_slot] = 1

        for a in range(row_slots):
            for b in range(col_slots):
                copy_of(k, a, b).start()
        return carry

    def copy_of(k, a, b):
        row = pl.multiple_of(starts_r[k, a] * strip, strip)
        col = pl.multiple_of(starts_c[k, b] * strip, strip)
        return pltpu.make_async_copy(
            ancestor.at[pl.ds(row, strip), pl.ds(col, strip)],
            tiles.at[k, pl.ds(a * strip, strip), pl.ds(b * strip, strip)],
            sems.at[k, a, b],
        )

    lax.fori_loop(0, supers, one, 0)
    for k in range(supers):
        for a in range(row_slots):
            for b in range(col_slots):
                copy_of(k, a, b).wait()


def main_kernel(rows, cols, halves, row_slots, col_slots,
                pick, rowq, tiles, panels, left, diag_inverse, upper, diag,
                own_tiles, mate_tiles, blocks, factor, factor_both, product, by_row, dense, by_pair, final,
                terms, mate_terms, by_pair_diag, tile_sem,
                s_mate, r_mate, s_block, r_block, s_factor, r_factor, s_row, r_row, s_pair, r_pair, s_final, r_final,
                s_term, r_term, s_dpair, r_dpair, s_out, r_out, s_last, r_last):
    supers, _, strip, width = panels.shape
    held = supers // 2
    waves = held * halves
    part = width // halves
    pairs = cols // 2
    sub = strip // rows
    slots = 2 * col_slots
    diag_rows = diag_inverse.shape[1]
    chunk = diag_rows // pairs
    r, c = lax.axis_index("row"), lax.axis_index("col")
    core = lax.rem(c, 2)
    pair = c // 2
    mate = c + 1 - 2 * core
    sends = []

    def send(src, dst, ssem, rsem, row, col):
        copy = pltpu.make_async_remote_copy(
            src_ref=src, dst_ref=dst, send_sem=ssem, recv_sem=rsem, device_id=(row, col), device_id_type=MESH)
        copy.start()
        sends.append(copy)

    def arrive(dst, ssem, rsem):
        pltpu.make_async_remote_copy(
            src_ref=dst, dst_ref=dst, send_sem=ssem, recv_sem=rsem, device_id=(r, mate), device_id_type=MESH).wait_recv()

    def turn(value, step, size):
        return lax.rem(value + step, size)

    def rows_of(index, size):
        return pl.ds(pl.multiple_of(index * size, size), size)

    def which(w, of_core):
        return of_core * held + w // halves, pl.ds((w % halves) * part, part)

    barrier = pltpu.get_barrier_semaphore()
    for d in range(1, cols):
        pl.semaphore_signal(barrier, inc=1, device_id=(r, turn(c, d, cols)), device_id_type=MESH)
    for d in range(1, rows):
        for col in (c, mate):
            pl.semaphore_signal(barrier, inc=1, device_id=(turn(r, d, rows), col), device_id_type=MESH)

    mine = rows_of(r, sub)
    own_copies = []
    for i in range(held):
        copy = pltpu.make_async_copy(tiles.at[core * held + i], own_tiles.at[i], tile_sem.at[i])
        copy.start()
        own_copies.append(copy)
    for w in range(waves):
        k, lanes = which(w, core)
        blocks[w][c] = panels[k, 0, mine, lanes]

    pl.semaphore_wait(barrier, cols - 1 + 2 * (rows - 1))

    for w in range(waves):
        for d in range(1, cols):
            col = turn(c, d, cols)
            k, lanes = which(w, lax.rem(col, 2))
            send(panels.at[k, 0, mine, lanes], blocks[w].at[c], s_block.at[w, d], r_block.at[w, c], r, col)
        if w % halves == 0:
            i = w // halves
            send(tiles.at[(1 - core) * held + i], mate_tiles.at[i], s_mate.at[i], r_mate.at[i], r, mate)

    def select(w):
        k, _ = which(w, core)
        for d in range(1, cols):
            source = turn(c, d, cols)
            arrive(blocks[w].at[source], s_block.at[w, d], r_block.at[w, source])
        for s in range(slots):
            factor[w, s, mine, :] = blocks[w][pick[k, s]] * pick[k, slots + s].astype(jnp.float32)
        for d in range(1, rows):
            share = factor.at[w, :, mine, :]
            send(share, share, s_factor.at[w, d], r_factor.at[w, r], turn(r, d, rows), c)

    half = col_slots * strip

    def multiply(w):
        i = w // halves
        for d in range(1, rows):
            source = turn(r, d, rows)
            arrive(factor.at[w, :, rows_of(source, sub), :], s_factor.at[w, d], r_factor.at[w, source])
        for s in range(slots):
            high, low = split(factor[w, s])
            factor_both[pl.ds(s * strip, strip), pl.ds(0, part)] = high
            factor_both[pl.ds(s * strip, strip), pl.ds(part, part)] = low
        if w % halves == 0:
            own_copies[i].wait()
            arrive(mate_tiles.at[i], s_mate.at[i], r_mate.at[i])

        def one(a, carry):
            band = rows_of(a, strip)
            total = None
            for first, source in ((0, own_tiles), (half, mate_tiles)):
                high, low = split(source[i, band, :])
                both = dot(high, factor_both[pl.ds(first, half), :])
                term = both[:, part:] + dot(low, factor_both[pl.ds(first, half), pl.ds(0, part)]) + both[:, :part]
                total = term if total is None else total + term
            product[w, a] = total
            return carry

        lax.fori_loop(0, row_slots, one, 0)
        for d in range(1, rows):
            target = turn(r, d, rows)
            send(product.at[w, :, rows_of(target, sub), :], by_row[w].at[pl.ds(r * row_slots, row_slots)],
                 s_row.at[w, d], r_row.at[w, r], target, c)
        by_row[w][pl.ds(r * row_slots, row_slots)] = product[w, :, mine, :]

    def scatter(w):
        k, _ = which(w, core)
        for d in range(1, rows):
            source = turn(r, d, rows)
            arrive(by_row[w].at[pl.ds(source * row_slots, row_slots)], s_row.at[w, d], r_row.at[w, source])
        for j in range(cols):
            dense[w, j] = -by_row[w][rowq[k, j]]
        for d in range(1, pairs):
            target = turn(pair, d, pairs)
            send(dense.at[w, pl.ds(target * 2, 2)], by_pair.at[w, pair], s_pair.at[w, d], r_pair.at[w, pair],
                 r, target * 2 + core)
        by_pair[w, pair] = dense[w, pl.ds(pair * 2, 2)]

    def spread(w):
        k, lanes = which(w, core)
        for d in range(1, pairs):
            source = turn(pair, d, pairs)
            arrive(by_pair.at[w, source], s_pair.at[w, d], r_pair.at[w, source])
        total = by_pair[w, 0]
        for z in range(1, pairs):
            total += by_pair[w, z]
        final[w] = total
        for d in range(rows):
            target = turn(r, d, rows)
            for e in range(2):
                if d or e:
                    col = mate if e else c
                    send(final.at[w, lax.rem(col, 2)], upper.at[k, 0, mine, lanes],
                         s_final.at[w, d, e], r_final.at[w, r, core], target, col)
        upper[k, 0, mine, lanes] = final[w, core]

    def term_of(w):
        for d in range(rows):
            source = turn(r, d, rows)
            for e in range(2):
                if d or e:
                    other = 1 - core if e else core
                    k, lanes = which(w, other)
                    arrive(upper.at[k, 0, rows_of(source, sub), lanes],
                           s_final.at[w, d, e], r_final.at[w, source, other])
        for e in range(2):
            k, lanes = which(w, e)
            l_high, l_low = split(left[k])
            u_high, u_low = split(upper[k, 0, :, lanes])
            terms[w, e] = dot_left(l_high, u_low) + dot_left(l_low, u_high) + dot_left(l_high, u_high)
        send(terms.at[w, 1 - core], mate_terms.at[w], s_term.at[w], r_term.at[w], r, mate)

    def term_scatter(w):
        arrive(mate_terms.at[w], s_term.at[w], r_term.at[w])
        mate_terms[w] = mate_terms[w] + terms[w, core]
        for d in range(1, pairs):
            target = turn(pair, d, pairs)
            send(mate_terms.at[w, rows_of(target, chunk), :], by_pair_diag.at[w, pair],
                 s_dpair.at[w, d], r_dpair.at[w, pair], r, target * 2 + core)
        by_pair_diag[w, pair] = mate_terms[w, rows_of(pair, chunk), :]

    def term_spread(w):
        k, lanes = which(w, core)
        for d in range(1, pairs):
            source = turn(pair, d, pairs)
            arrive(by_pair_diag.at[w, source], s_dpair.at[w, d], r_dpair.at[w, source])
        total = by_pair_diag[w, 0]
        for z in range(1, pairs):
            total += by_pair_diag[w, z]
        place = rows_of(pair, chunk)
        diag[k, place, lanes] = diag_inverse[k, place, lanes] - total
        share = diag.at[k, place, lanes]
        for d in range(1, pairs):
            send(share, share, s_out.at[w, d], r_out.at[w, pair], r, turn(pair, d, pairs) * 2 + core)

    def hand_over(w):
        k, lanes = which(w, core)
        for d in range(1, pairs):
            source = turn(pair, d, pairs)
            arrive(diag.at[k, rows_of(source, chunk), lanes], s_out.at[w, d], r_out.at[w, source])
        share = diag.at[k, :, lanes]
        send(share, share, s_last.at[w], r_last.at[w], r, mate)

    def last(w):
        k, lanes = which(w, 1 - core)
        arrive(diag.at[k, :, lanes], s_last.at[w], r_last.at[w])

    stages = ((select, 0, 67), (multiply, 41, 87), (scatter, 72, 99), (spread, 83, 110), (term_of, 96, 132),
              (term_scatter, 97, 133), (term_spread, 108, 153), (hand_over, 144, 220), (last, 147, 281))
    order = [
        (first + (end - first) * w / max(1, waves - 1), stage, w) for stage, first, end in stages for w in range(waves)
    ]
    for _, stage, w in sorted(order, key=lambda item: item[0]):
        stage(w)
    for copy in sends:
        copy.wait_send()


def local(ancestor, panels, diag_inverse, fill_strips):
    supers, local_fill, strip, width = panels.shape
    rows, cols = lax.axis_size("row"), lax.axis_size("col")
    fill = fill_strips.shape[1]
    row_slots = 2 * local_fill * cols // rows
    col_slots = 2 * local_fill
    row_strips, col_strips = ancestor.shape[0] // strip, ancestor.shape[1] // strip
    halves = max(1, width // 256)
    held, part = supers // 2, width // halves
    waves, pairs, sub, slots = held * halves, cols // 2, strip // rows, 2 * col_slots
    diag_rows = diag_inverse.shape[1]
    chunk = diag_rows // pairs
    f32, i32, bf16 = jnp.float32, jnp.int32, jnp.bfloat16
    smem, vmem, anywhere = (pl.BlockSpec(memory_space=m) for m in (pltpu.SMEM, pltpu.VMEM, pl.ANY))
    dma = pltpu.SemaphoreType.DMA
    tiles, pick, rowq = pl.pallas_call(
        functools.partial(gather_kernel, row_slots, col_slots, strip, row_strips, col_strips),
        out_shape=(
            jax.ShapeDtypeStruct((supers, row_slots * strip, col_slots * strip), f32),
            jax.ShapeDtypeStruct((supers, 2 * slots), i32),
            jax.ShapeDtypeStruct((supers, fill), i32),
        ),
        in_specs=[smem, anywhere],
        out_specs=(vmem, smem, smem),
        scratch_shapes=[
            pltpu.SMEM((supers, row_slots), i32),
            pltpu.SMEM((supers, col_slots), i32),
            dma((supers, row_slots, col_slots)),
        ],
        compiler_params=pltpu.CompilerParams(vmem_limit_bytes=56 * 2**20),
        name="pick_tiles",
    )(fill_strips, ancestor)
    left = lax.dynamic_slice_in_dim(panels[:, 0], lax.axis_index("row") * diag_rows, diag_rows, 2)
    return pl.pallas_call(
        functools.partial(main_kernel, rows, cols, halves, row_slots, col_slots),
        out_shape=(
            jax.ShapeDtypeStruct(panels.shape, f32),
            jax.ShapeDtypeStruct(diag_inverse.shape, f32),
        ),
        in_specs=[smem, smem, anywhere, vmem, vmem, vmem],
        out_specs=(vmem, vmem),
        scratch_shapes=[
            pltpu.VMEM((held, row_slots * strip, col_slots * strip), f32),
            pltpu.VMEM((held, row_slots * strip, col_slots * strip), f32),
            [pltpu.VMEM((cols, sub, part), f32)] * waves,
            pltpu.VMEM((waves, slots, strip, part), f32),
            pltpu.VMEM((slots * strip, 2 * part), bf16),
            pltpu.VMEM((waves, row_slots, strip, part), f32),
            [pltpu.VMEM((rows * row_slots, sub, part), f32)] * waves,
            pltpu.VMEM((waves, cols, sub, part), f32),
            pltpu.VMEM((waves, pairs, 2, sub, part), f32),
            pltpu.VMEM((waves, 2, sub, part), f32),
            pltpu.VMEM((waves, 2, diag_rows, part), f32),
            pltpu.VMEM((waves, diag_rows, part), f32),
            pltpu.VMEM((waves, pairs, chunk, part), f32),
            dma((held,)),
            dma((held,)), dma((held,)),
            dma((waves, cols)), dma((waves, cols)),
            dma((waves, rows)), dma((waves, rows)),
            dma((waves, rows)), dma((waves, rows)),
            dma((waves, pairs)), dma((waves, pairs)),
            dma((waves, rows, 2)), dma((waves, rows, 2)),
            dma((waves,)), dma((waves,)),
            dma((waves, pairs)), dma((waves, pairs)),
            dma((waves, pairs)), dma((waves, pairs)),
            dma((waves,)), dma((waves,)),
        ],
        compiler_params=pltpu.CompilerParams(
            collective_id=0, has_side_effects=True, vmem_limit_bytes=56 * 2**20),
        name="update",
    )(pick, rowq, tiles, panels, left, diag_inverse)


def solution(mesh):
    return jax.shard_map(
        local,
        mesh=mesh,
        in_specs=(P("row", "col"), P(None, "col", None, None), P(None, "row", None), P()),
        out_specs=(P(None, "col", None, None), P(None, "row", None)),
        check_vma=False,
    )
```
